32 devices in a mesh: read: 4 (over y, x), row: 8 (over z, core).
Axes of the slice: x: 2, y: 2, z: 4, core: 2. Of those that a mesh axis runs over, the one named last changes fastest.
Arguments:
- snapshots: float32 [256, 40960], P(('read', 'row')), may hold values from -400 to 400
- coefficients: float32 [256, 256], replicated, may hold values from -0.375 to 0.375
Outputs:
- modes: float32 [256, 40960], P(('read', 'row'))
The draws below stay inside these ranges and needn't reach their ends.
All inputs are finite; a program needn't handle non-finite values.
Results may differ from the reference program's by a relative error of at most 0.000078.
Values sent between devices are 32-bit elements; how exact they have to be, the bound alone decides.
A program may use at most 192 MiB of HBM per device.

```python
import math
import jax
import jax.numpy as jnp
from jax import lax

SNAPS = 256
MODES = 256
ROWS = 40960


def draw_snapshots(key, part):
    key = jax.random.fold_in(key, 11)
    key_noise, key_rough, key_column = jax.random.split(key, 3)
    height = jnp.arange(ROWS, dtype=jnp.float32) / ROWS
    profile = jnp.exp(math.log(4.0) * height) * jax.random.uniform(key_rough, (ROWS,), jnp.float32, 0.5, 1.5)
    fluctuation = jnp.clip(jax.random.normal(key_noise, (SNAPS, ROWS), jnp.float32), -6.0, 6.0)
    column_scale = jnp.exp(jax.random.uniform(key_column, (SNAPS, 1), jnp.float32, 0.0, math.log(10.0)))
    values_out = fluctuation * column_scale * profile[None, :]
    return values_out


def normal_values(stream_key, shape, scale, limit, held_as=jnp.bfloat16):
    array = jax.random.normal(stream_key, shape, jnp.float32) * scale
    return jnp.minimum(jnp.maximum(array, -limit), limit).astype(held_as)


def setup_inputs(seed: int = 0) -> dict:
    keys = jax.random.split(jax.random.key(seed), 3)
    return {
        "snapshots": draw_snapshots(jax.random.fold_in(keys[2], 71), 0),
        "coefficients": normal_values(keys[1], (SNAPS, MODES), SNAPS ** -0.5, 0.375, jnp.float32),
    }


def reference(snapshots, coefficients):
    gram_matrix = lax.dot_general(snapshots.astype(jnp.float32), snapshots.astype(jnp.float32), (((1,), (1,)), ((), ())), precision=lax.Precision.HIGHEST, preferred_element_type=jnp.float32)
    upper_factor = jnp.linalg.cholesky(gram_matrix).T
    folded = lax.linalg.triangular_solve(upper_factor, coefficients, left_side=True, lower=False)
    row_scale = math.sqrt(ROWS)
    product = jnp.dot(folded.T.astype(jnp.float32), snapshots.astype(jnp.float32), precision=lax.Precision.HIGHEST, preferred_element_type=jnp.float32)
    return row_scale * product
```

```python
import functools
import math

import jax
import jax.numpy as jnp
from jax import lax
from jax.experimental import pallas as pl
from jax.experimental.pallas import tpu as pltpu
from jax.sharding import PartitionSpec as P

AXES = ("read", "row")
HIGHEST = lax.Precision.HIGHEST
NN = (((1,), (0,)), ((), ()))
NT = (((1,), (1,)), ((), ()))
VMEM_BYTES = 48 * 1024 * 1024


def product(left, right, dims=NN):
    return lax.dot_general(left, right, dims, precision=HIGHEST, preferred_element_type=jnp.float32)


def position(count_row):
    return lax.axis_index("read") * count_row + lax.axis_index("row")


def coordinates(index, count_row):
    return (lax.div(index, count_row), lax.rem(index, count_row))


def greet(count, count_row, me):
    barrier = pltpu.get_barrier_semaphore()

    def signal(offset, carry):
        other = lax.rem(me + offset, count)
        pl.semaphore_signal(
            barrier, inc=1, device_id=coordinates(other, count_row), device_id_type=pl.DeviceIdType.MESH
        )
        return carry

    lax.fori_loop(1, count, signal, 0)
    return barrier


def wait_bytes(ref, semaphore):
    pltpu.make_async_copy(ref, ref, semaphore).wait()


def gram_kernel(count, count_row, chunks, snap_ref, gram_ref, held_ref, part, slabs,
                local_sem, send_sem, recv_sem):
    me = position(count_row)
    share = snap_ref.shape[0]
    width = held_ref.shape[1]
    piece = width // chunks
    others = (count - 1) * share
    barrier = greet(count, count_row, me)
    mine = pl.ds(pl.multiple_of(me * share, share), share)
    own = pltpu.make_async_copy(
        snap_ref.at[:, pl.ds(pl.multiple_of(me * width, width), width)], held_ref.at[mine, :], local_sem
    )
    own.start()
    pl.semaphore_wait(barrier, count - 1)

    def send(source, target, other, stage):
        pltpu.make_async_remote_copy(
            src_ref=source,
            dst_ref=target,
            send_sem=send_sem.at[stage],
            recv_sem=recv_sem.at[stage],
            device_id=coordinates(other, count_row),
            device_id_type=pl.DeviceIdType.MESH,
        ).start()

    for chunk in range(chunks):
        def scatter(offset, carry, chunk=chunk):
            other = lax.rem(me + offset, count)
            send(
                snap_ref.at[:, pl.ds(pl.multiple_of(other * width + chunk * piece, 128), piece)],
                held_ref.at[mine, pl.ds(chunk * piece, piece)],
                other,
                chunk,
            )
            return carry

        lax.fori_loop(1, count, scatter, 0)

    own.wait()
    for chunk in range(chunks):
        columns = pl.ds(chunk * piece, piece)
        wait_bytes(held_ref.at[pl.ds(0, others), columns], recv_sem.at[chunk])
        block = held_ref[:, columns]
        term = product(block, block, NT)
        if chunk:
            part[...] += term
        else:
            part[...] = term

    slabs[pl.ds(me, 1)] = part[mine, :][None]

    def scatter_part(offset, carry):
        other = lax.rem(me + offset, count)
        rows = pl.ds(pl.multiple_of(other * share, share), share)
        send(part.at[rows, :], slabs.at[me], other, chunks)
        return carry

    lax.fori_loop(1, count, scatter_part, 0)
    wait_bytes(part.at[pl.ds(0, others), :], recv_sem.at[chunks])
    gram_ref[mine, :] = jnp.sum(slabs[...], axis=0)

    def share_total(offset, carry):
        other = lax.rem(me + offset, count)
        send(gram_ref.at[mine, :], gram_ref.at[mine, :], other, chunks + 1)
        return carry

    lax.fori_loop(1, count, share_total, 0)
    wait_bytes(part.at[pl.ds(0, others), :], recv_sem.at[chunks + 1])
    for chunk in range(chunks):
        wait_bytes(held_ref.at[pl.ds(0, others), pl.ds(0, piece)], send_sem.at[chunk])
    wait_bytes(part.at[pl.ds(0, others), :], send_sem.at[chunks])
    wait_bytes(part.at[pl.ds(0, others), :], send_sem.at[chunks + 1])


def modes_kernel(count, count_row, groups, fold_ref, held_ref, out_ref, modes, local_sem, send_sem, recv_sem):
    me = position(count_row)
    snaps, width = held_ref.shape
    share = out_ref.shape[0]
    rows = snaps // groups
    dests = rows // share
    barrier = greet(count, count_row, me)
    target = pl.ds(pl.multiple_of(me * width, width), width)
    first = lax.div(me, dests)

    for step in range(groups):
        group = lax.rem(first + step, groups)
        span = pl.ds(pl.multiple_of(group * rows, rows), rows)
        modes[span, :] = product(fold_ref[span, :], held_ref[...])
        if step == 0:
            own = pltpu.make_async_copy(
                modes.at[pl.ds(pl.multiple_of(me * share, share), share), :], out_ref.at[:, target], local_sem
            )
            own.start()
            pl.semaphore_wait(barrier, count - 1)

        def scatter(offset, carry):
            other = group * dests + lax.rem(lax.rem(me, dests) + offset, dests)
            pltpu.make_async_remote_copy(
                src_ref=modes.at[pl.ds(pl.multiple_of(other * share, share), share), :],
                dst_ref=out_ref.at[:, target],
                send_sem=send_sem,
                recv_sem=recv_sem,
                device_id=coordinates(other, count_row),
                device_id_type=pl.DeviceIdType.MESH,
            ).start()
            return carry

        lax.fori_loop(1 if step == 0 else 0, dests, scatter, 0)

    others = modes.at[pl.ds(0, (count - 1) * share), :]
    own.wait()
    wait_bytes(others, recv_sem)
    wait_bytes(others, send_sem)


def eliminate(block):
    size = block.shape[0]
    row_id = lax.broadcasted_iota(jnp.int32, (size, 2 * size), 0)
    col_id = lax.broadcasted_iota(jnp.int32, (size, 2 * size), 1)
    state = jnp.concatenate([block, jnp.zeros_like(block)], axis=1)
    state = jnp.where(col_id == row_id + size, 1.0, state)
    for k in range(size - 1):
        pivot_row = state[k : k + 1, :]
        inverse = 1.0 / state[k : k + 1, k : k + 1]
        scaled = pivot_row * inverse
        low = (k + 1) // 8 * 8
        below = state[low:, :]
        column = below[:, k : k + 1]
        if low <= k:
            column = jnp.where(row_id[low:, :1] > k, column, 0.0)
        below = below - column * scaled
        state = jnp.concatenate([state[:low], below], axis=0) if low else below
    pivots = jnp.sum(jnp.where(col_id == row_id, state, 0.0), axis=1, keepdims=True)
    return state[:, size:] * lax.rsqrt(pivots)


def factor_kernel(size, scale, gram_ref, coef_ref, fold_ref, work, inverse):
    total = gram_ref.shape[0]
    blocks = total // size
    work[...] = gram_ref[...]
    inverse[...] = jnp.zeros_like(inverse)
    for k in range(blocks):
        here = slice(k * size, (k + 1) * size)
        low = eliminate(work[here, here])
        before = slice(0, k * size)
        after = slice((k + 1) * size, total)
        if k:
            inverse[here, before] = product(low, inverse[here, before])
        inverse[here, here] = low
        if k < blocks - 1:
            across = product(low, work[here, after])
            down = product(work[after, here], low, NT)
            work[after, after] -= product(down, across)
            inverse[after, slice(0, (k + 1) * size)] -= product(down, inverse[here, slice(0, (k + 1) * size)])
    fold_ref[...] = scale * lax.dot_general(
        coef_ref[...], inverse[...], (((0,), (0,)), ((), ())),
        precision=HIGHEST, preferred_element_type=jnp.float32,
    )


def vmem_spec():
    return pl.BlockSpec(memory_space=pltpu.VMEM)


def any_spec():
    return pl.BlockSpec(memory_space=pl.ANY)


def cost(flops, moved):
    return pl.CostEstimate(flops=flops, bytes_accessed=moved, transcendentals=0)


def factor(gram, coefficients, scale):
    snaps = gram.shape[0]
    return pl.pallas_call(
        functools.partial(factor_kernel, 64, scale),
        out_shape=jax.ShapeDtypeStruct((coefficients.shape[1], snaps), jnp.float32),
        in_specs=[vmem_spec()] * 2,
        out_specs=vmem_spec(),
        scratch_shapes=[pltpu.VMEM((snaps, snaps), jnp.float32)] * 2,
        compiler_params=pltpu.CompilerParams(vmem_limit_bytes=VMEM_BYTES),
        cost_estimate=cost(6 * snaps**3, 12 * snaps**2),
        name="factor",
    )(gram, coefficients)


def direct(snapshots, coefficients, count, count_row):
    share, total_rows = snapshots.shape
    snaps, width = share * count, total_rows // count
    chunks = 2 if width % 256 == 0 else 1
    gram, held = pl.pallas_call(
        functools.partial(gram_kernel, count, count_row, chunks),
        out_shape=(
            jax.ShapeDtypeStruct((snaps, snaps), jnp.float32),
            jax.ShapeDtypeStruct((snaps, width), jnp.float32),
        ),
        in_specs=[any_spec()],
        out_specs=(vmem_spec(), vmem_spec()),
        scratch_shapes=[
            pltpu.VMEM((snaps, snaps), jnp.float32),
            pltpu.VMEM((count, share, snaps), jnp.float32),
            pltpu.SemaphoreType.DMA,
            pltpu.SemaphoreType.DMA((chunks + 2,)),
            pltpu.SemaphoreType.DMA((chunks + 2,)),
        ],
        compiler_params=pltpu.CompilerParams(
            collective_id=0, has_side_effects=True, vmem_limit_bytes=VMEM_BYTES
        ),
        cost_estimate=cost(2 * snaps * snaps * width, 8 * snaps * width),
        name="gram",
    )(snapshots)
    folded = factor(gram, coefficients, math.sqrt(total_rows))
    return pl.pallas_call(
        functools.partial(modes_kernel, count, count_row, 4),
        out_shape=jax.ShapeDtypeStruct((share, total_rows), jnp.float32),
        in_specs=[vmem_spec(), vmem_spec()],
        out_specs=any_spec(),
        scratch_shapes=[
            pltpu.VMEM((snaps, width), jnp.float32),
            pltpu.SemaphoreType.DMA,
            pltpu.SemaphoreType.DMA,
            pltpu.SemaphoreType.DMA,
        ],
        compiler_params=pltpu.CompilerParams(
            collective_id=1, has_side_effects=True, vmem_limit_bytes=VMEM_BYTES
        ),
        cost_estimate=cost(2 * snaps * snaps * width, 8 * snaps * width),
        name="modes",
    )(folded, held)


def shards(snapshots, coefficients):
    count_row = lax.axis_size("row")
    count = lax.axis_size("read") * count_row
    if snapshots.shape[0] % 8 == 0 and count % 4 == 0:
        return direct(snapshots, coefficients, count, count_row)
    held = lax.all_to_all(snapshots, AXES, split_axis=1, concat_axis=0, tiled=True)
    gram = lax.psum(product(held, held, NT), AXES)
    folded = factor(gram, coefficients, math.sqrt(snapshots.shape[1]))
    return lax.all_to_all(product(folded, held), AXES, split_axis=0, concat_axis=1, tiled=True)


def solution(mesh):
    in_specs = (P(AXES, None), P())
    out_specs = P(AXES, None)
    return jax.shard_map(shards, mesh=mesh, in_specs=in_specs, out_specs=out_specs, check_vma=False)
```

```python
import functools
import math

import jax
import jax.numpy as jnp
from jax import lax
from jax.experimental import pallas as pl
from jax.experimental.pallas import tpu as pltpu
from jax.sharding import PartitionSpec as P

AXES = ("read", "row")
HIGHEST = lax.Precision.HIGHEST
NN = (((1,), (0,)), ((), ()))
NT = (((1,), (1,)), ((), ()))
VMEM_BYTES = 60 * 1024 * 1024
GROUP = 16


def product(left, right, dims=NN):
    return lax.dot_general(left, right, dims, precision=HIGHEST, preferred_element_type=jnp.float32)


def position(count_row):
    return lax.axis_index("read") * count_row + lax.axis_index("row")


def coordinates(index, count_row):
    return (lax.div(index, count_row), lax.rem(index, count_row))


def greet(count, count_row, me):
    barrier = pltpu.get_barrier_semaphore()

    def signal(offset, carry):
        other = lax.rem(me + offset, count)
        pl.semaphore_signal(
            barrier, inc=1, device_id=coordinates(other, count_row), device_id_type=pl.DeviceIdType.MESH
        )
        return carry

    lax.fori_loop(1, count, signal, 0)
    return barrier


def wait_bytes(ref, semaphore):
    pltpu.make_async_copy(ref, ref, semaphore).wait()


def gram_kernel(count, count_row, chunks, snap_ref, gram_ref, held_ref, part, slabs,
                local_sem, send_sem, recv_sem):
    me = position(count_row)
    share = snap_ref.shape[0]
    width = held_ref.shape[1]
    piece = width // chunks
    others = (count - 1) * share
    barrier = greet(count, count_row, me)
    mine = pl.ds(pl.multiple_of(me * share, share), share)
    own = pltpu.make_async_copy(
        snap_ref.at[:, pl.ds(pl.multiple_of(me * width, width), width)], held_ref.at[mine, :], local_sem
    )
    own.start()
    pl.semaphore_wait(barrier, count - 1)

    def send(source, target, other, stage):
        pltpu.make_async_remote_copy(
            src_ref=source,
            dst_ref=target,
            send_sem=send_sem.at[stage],
            recv_sem=recv_sem.at[stage],
            device_id=coordinates(other, count_row),
            device_id_type=pl.DeviceIdType.MESH,
        ).start()

    for chunk in range(chunks):
        def scatter(offset, carry, chunk=chunk):
            other = lax.rem(me + offset, count)
            send(
                snap_ref.at[:, pl.ds(pl.multiple_of(other * width + chunk * piece, 128), piece)],
                held_ref.at[mine, pl.ds(chunk * piece, piece)],
                other,
                chunk,
            )
            return carry

        lax.fori_loop(1, count, scatter, 0)

    own.wait()
    for chunk in range(chunks):
        columns = pl.ds(chunk * piece, piece)
        wait_bytes(held_ref.at[pl.ds(0, others), columns], recv_sem.at[chunk])
        block = held_ref[:, columns]
        term = product(block, block, NT)
        if chunk:
            part[...] += term
        else:
            part[...] = term

    slabs[pl.ds(me, 1)] = part[mine, :][None]

    def scatter_part(offset, carry):
        other = lax.rem(me + offset, count)
        rows = pl.ds(pl.multiple_of(other * share, share), share)
        send(part.at[rows, :], slabs.at[me], other, chunks)
        return carry

    lax.fori_loop(1, count, scatter_part, 0)
    wait_bytes(part.at[pl.ds(0, others), :], recv_sem.at[chunks])
    gram_ref[mine, :] = jnp.sum(slabs[...], axis=0)

    def share_total(offset, carry):
        other = lax.rem(me + offset, count)
        send(gram_ref.at[mine, :], gram_ref.at[mine, :], other, chunks + 1)
        return carry

    lax.fori_loop(1, count, share_total, 0)
    wait_bytes(part.at[pl.ds(0, others), :], recv_sem.at[chunks + 1])
    for chunk in range(chunks):
        wait_bytes(held_ref.at[pl.ds(0, others), pl.ds(0, piece)], send_sem.at[chunk])
    wait_bytes(part.at[pl.ds(0, others), :], send_sem.at[chunks])
    wait_bytes(part.at[pl.ds(0, others), :], send_sem.at[chunks + 1])


def modes_kernel(count, count_row, groups, fold_ref, held_ref, out_ref, modes, local_sem, send_sem, recv_sem):
    me = position(count_row)
    snaps, width = held_ref.shape
    share = out_ref.shape[0]
    rows = snaps // groups
    dests = rows // share
    barrier = greet(count, count_row, me)
    target = pl.ds(pl.multiple_of(me * width, width), width)
    first = lax.div(me, dests)

    for step in range(groups):
        group = lax.rem(first + step, groups)
        span = pl.ds(pl.multiple_of(group * rows, rows), rows)
        modes[span, :] = product(fold_ref[span, :], held_ref[...])
        if step == 0:
            own = pltpu.make_async_copy(
                modes.at[pl.ds(pl.multiple_of(me * share, share), share), :], out_ref.at[:, target], local_sem
            )
            own.start()
            pl.semaphore_wait(barrier, count - 1)

        def scatter(offset, carry):
            other = group * dests + lax.rem(lax.rem(me, dests) + offset, dests)
            pltpu.make_async_remote_copy(
                src_ref=modes.at[pl.ds(pl.multiple_of(other * share, share), share), :],
                dst_ref=out_ref.at[:, target],
                send_sem=send_sem,
                recv_sem=recv_sem,
                device_id=coordinates(other, count_row),
                device_id_type=pl.DeviceIdType.MESH,
            ).start()
            return carry

        lax.fori_loop(1 if step == 0 else 0, dests, scatter, 0)

    others = modes.at[pl.ds(0, (count - 1) * share), :]
    own.wait()
    wait_bytes(others, recv_sem)
    wait_bytes(others, send_sem)


def eliminate(block):
    size = block.shape[0]
    row_id = lax.broadcasted_iota(jnp.int32, (size, 2 * size), 0)
    col_id = lax.broadcasted_iota(jnp.int32, (size, 2 * size), 1)
    active = jnp.concatenate([block, jnp.zeros_like(block)], axis=1)
    active = jnp.where(col_id == row_id + size, 1.0, active)
    done = []
    for start in range(0, size, GROUP):
        below = row_id[: size - start]
        columns = [
            jnp.broadcast_to(active[:, start + j : start + j + 1], active.shape) for j in range(GROUP)
        ]
        for j in range(GROUP):
            inverse = 1.0 / columns[j][j : j + 1, :]
            ratio = jnp.where(below > j, columns[j] * inverse, 0.0)
            for i in range(j + 1, GROUP):
                columns[i] = columns[i] - ratio * columns[i][j : j + 1, :]
            active = active - ratio * active[j : j + 1, :]
        done.append(active[:GROUP])
        active = active[GROUP:]
    state = jnp.concatenate(done, axis=0)
    pivots = jnp.sum(jnp.where(col_id == row_id, state, 0.0), axis=1, keepdims=True)
    return state[:, size:] * lax.rsqrt(pivots)


def factor_kernel(size, scale, gram_ref, coef_ref, fold_ref, work, inverse):
    total = gram_ref.shape[0]
    blocks = total // size
    work[...] = gram_ref[...]
    inverse[...] = jnp.zeros_like(inverse)
    for k in range(blocks):
        here = slice(k * size, (k + 1) * size)
        low = eliminate(work[here, here])
        before = slice(0, k * size)
        after = slice((k + 1) * size, total)
        if k:
            inverse[here, before] = product(low, inverse[here, before])
        inverse[here, here] = low
        if k < blocks - 1:
            across = product(low, work[here, after])
            down = product(work[after, here], low, NT)
            work[after, after] -= product(down, across)
            inverse[after, slice(0, (k + 1) * size)] -= product(down, inverse[here, slice(0, (k + 1) * size)])
    fold_ref[...] = scale * lax.dot_general(
        coef_ref[...], inverse[...], (((0,), (0,)), ((), ())),
        precision=HIGHEST, preferred_element_type=jnp.float32,
    )


def vmem_spec():
    return pl.BlockSpec(memory_space=pltpu.VMEM)


def any_spec():
    return pl.BlockSpec(memory_space=pl.ANY)


def cost(flops, moved):
    return pl.CostEstimate(flops=flops, bytes_accessed=moved, transcendentals=0)


def factor(gram, coefficients, scale):
    snaps = gram.shape[0]
    return pl.pallas_call(
        functools.partial(factor_kernel, 64, scale),
        out_shape=jax.ShapeDtypeStruct((coefficients.shape[1], snaps), jnp.float32),
        in_specs=[vmem_spec()] * 2,
        out_specs=vmem_spec(),
        scratch_shapes=[pltpu.VMEM((snaps, snaps), jnp.float32)] * 2,
        compiler_params=pltpu.CompilerParams(vmem_limit_bytes=VMEM_BYTES),
        cost_estimate=cost(6 * snaps**3, 12 * snaps**2),
        name="factor",
    )(gram, coefficients)


def direct(snapshots, coefficients, count, count_row):
    share, total_rows = snapshots.shape
    snaps, width = share * count, total_rows // count
    chunks = 2 if width % 256 == 0 else 1
    gram, held = pl.pallas_call(
        functools.partial(gram_kernel, count, count_row, chunks),
        out_shape=(
            jax.ShapeDtypeStruct((snaps, snaps), jnp.float32),
            jax.ShapeDtypeStruct((snaps, width), jnp.float32),
        ),
        in_specs=[any_spec()],
        out_specs=(vmem_spec(), vmem_spec()),
        scratch_shapes=[
            pltpu.VMEM((snaps, snaps), jnp.float32),
            pltpu.VMEM((count, share, snaps), jnp.float32),
            pltpu.SemaphoreType.DMA,
            pltpu.SemaphoreType.DMA((chunks + 2,)),
            pltpu.SemaphoreType.DMA((chunks + 2,)),
        ],
        compiler_params=pltpu.CompilerParams(
            collective_id=0, has_side_effects=True, vmem_limit_bytes=VMEM_BYTES
        ),
        cost_estimate=cost(2 * snaps * snaps * width, 8 * snaps * width),
        name="gram",
    )(snapshots)
    folded = factor(gram, coefficients, math.sqrt(total_rows))
    return pl.pallas_call(
        functools.partial(modes_kernel, count, count_row, 4),
        out_shape=jax.ShapeDtypeStruct((share, total_rows), jnp.float32),
        in_specs=[vmem_spec(), vmem_spec()],
        out_specs=any_spec(),
        scratch_shapes=[
            pltpu.VMEM((snaps, width), jnp.float32),
            pltpu.SemaphoreType.DMA,
            pltpu.SemaphoreType.DMA,
            pltpu.SemaphoreType.DMA,
        ],
        compiler_params=pltpu.CompilerParams(
            collective_id=1, has_side_effects=True, vmem_limit_bytes=VMEM_BYTES
        ),
        cost_estimate=cost(2 * snaps * snaps * width, 8 * snaps * width),
        name="modes",
    )(folded, held)


def shards(snapshots, coefficients):
    count_row = lax.axis_size("row")
    count = lax.axis_size("read") * count_row
    if snapshots.shape[0] % 8 == 0 and count % 4 == 0:
        return direct(snapshots, coefficients, count, count_row)
    held = lax.all_to_all(snapshots, AXES, split_axis=1, concat_axis=0, tiled=True)
    gram = lax.psum(product(held, held, NT), AXES)
    folded = factor(gram, coefficients, math.sqrt(snapshots.shape[1]))
    return lax.all_to_all(product(folded, held), AXES, split_axis=0, concat_axis=1, tiled=True)


def solution(mesh):
    in_specs = (P(AXES, None), P())
    out_specs = P(AXES, None)
    return jax.shard_map(shards, mesh=mesh, in_specs=in_specs, out_specs=out_specs, check_vma=False)
```

```python
import functools
import math

import jax
import jax.numpy as jnp
from jax import lax
from jax.experimental import pallas as pl
from jax.experimental.pallas import tpu as pltpu
from jax.sharding import PartitionSpec as P

AXES = ("read", "row")
HIGHEST = lax.Precision.HIGHEST
NN = (((1,), (0,)), ((), ()))
NT = (((1,), (1,)), ((), ()))
VMEM_BYTES = 60 * 1024 * 1024
GROUP = 16
BLOCK = 64


def product(left, right, dims=NN):
    return lax.dot_general(left, right, dims, precision=HIGHEST, preferred_element_type=jnp.float32)


def coordinates(index, count_row):
    return (lax.div(index, count_row), lax.rem(index, count_row))


def greet(count, count_row, me):
    barrier = pltpu.get_barrier_semaphore()

    def signal(offset, carry):
        other = lax.rem(me + offset, count)
        pl.semaphore_signal(
            barrier, inc=1, device_id=coordinates(other, count_row), device_id_type=pl.DeviceIdType.MESH
        )
        return carry

    lax.fori_loop(1, count, signal, 0)
    return barrier


def wait_bytes(ref, semaphore):
    pltpu.make_async_copy(ref, ref, semaphore).wait()


def modes_kernel(count, count_row, chunks, size, scale, snap_ref, coef_ref, out_ref,
                 held, twin, part, slabs, levels, gram, work, inverse, fold, modes,
                 local_sem, send_sem, recv_sem):
    share = snap_ref.shape[0]
    snaps, width = held.shape
    piece = width // chunks
    half_row = count_row // 2
    half = count // 2
    layers = count_row // 2
    plane = count // layers
    strip = snaps // plane
    read, row = lax.axis_index("read"), lax.axis_index("row")
    me = read * count_row + row
    side = lax.div(row, half_row)
    partner = read * count_row + lax.rem(row + half_row, count_row)
    place = read * half_row + lax.rem(row, half_row)
    layer, core = lax.div(row, 2), lax.rem(row, 2)
    spot = read * 2 + core

    def rows_of(index, length):
        return pl.ds(pl.multiple_of(index * length, length), length)

    def columns_of(index):
        return pl.ds(pl.multiple_of(index * width, width), width)

    def in_half(index):
        return lax.div(index, half_row) * count_row + side * half_row + lax.rem(index, half_row)

    def mirrored(device):
        other_row = lax.rem(lax.rem(device, count_row) + half_row, count_row)
        return lax.div(device, count_row) * count_row + other_row

    def slab_of(column, which):
        start = (column * count_row + which * half_row) * share
        return pl.ds(pl.multiple_of(start, share), half_row * share)

    def send(source, target, other, stage):
        pltpu.make_async_remote_copy(
            src_ref=source,
            dst_ref=target,
            send_sem=send_sem.at[stage],
            recv_sem=recv_sem.at[stage],
            device_id=coordinates(other, count_row),
            device_id_type=pl.DeviceIdType.MESH,
        ).start()

    mine = rows_of(me, share)
    twin_stage, fetch_stage, scatter_stage, layer_stage, share_stage, out_stage = range(chunks, chunks + 6)

    barrier = greet(count, count_row, me)
    own = pltpu.make_async_copy(snap_ref.at[:, columns_of(me)], held.at[mine, :], local_sem.at[0])
    own.start()
    own_twin = pltpu.make_async_copy(snap_ref.at[:, columns_of(partner)], twin.at[mine, :], local_sem.at[1])
    own_twin.start()
    pl.semaphore_wait(barrier, count - 1)

    for chunk in range(chunks):
        def scatter(offset, carry, chunk=chunk):
            other = lax.rem(me + offset, count)
            send(
                snap_ref.at[:, pl.ds(pl.multiple_of(other * width + chunk * piece, 128), piece)],
                held.at[mine, pl.ds(chunk * piece, piece)],
                other,
                chunk,
            )
            return carry

        lax.fori_loop(1, count, scatter, 0)

    def scatter_twin(offset, carry):
        other = in_half(lax.rem(place + offset, half))
        send(snap_ref.at[:, columns_of(mirrored(other))], twin.at[mine, :], other, twin_stage)
        return carry

    lax.fori_loop(1, half, scatter_twin, 0)

    own.wait()
    for chunk in range(chunks):
        columns = pl.ds(chunk * piece, piece)
        wait_bytes(held.at[pl.ds(0, (count - 1) * share), columns], recv_sem.at[chunk])
        block = held[:, columns]
        term = product(block, block, NT)
        if chunk:
            part[...] += term
        else:
            part[...] = term

    for column in range(count // count_row):
        slab = slab_of(column, side)
        send(held.at[slab, :], twin.at[slab, :], partner, fetch_stage)

    slabs[pl.ds(spot, 1)] = part[rows_of(spot, strip), :][None]

    def at_spot(index):
        return lax.div(index, 2) * count_row + layer * 2 + lax.rem(index, 2)

    def scatter_part(offset, carry):
        index = lax.rem(spot + offset, plane)
        send(part.at[rows_of(index, strip), :], slabs.at[spot], at_spot(index), scatter_stage)
        return carry

    lax.fori_loop(1, plane, scatter_part, 0)
    wait_bytes(part.at[pl.ds(0, (plane - 1) * strip), :], recv_sem.at[scatter_stage])
    levels[pl.ds(layer, 1)] = jnp.sum(slabs[...], axis=0)[None]

    def exchange_layer(offset, carry):
        index = lax.rem(layer + offset, layers)
        send(levels.at[layer], levels.at[layer], read * count_row + index * 2 + core, layer_stage)
        return carry

    lax.fori_loop(1, layers, exchange_layer, 0)
    wait_bytes(part.at[pl.ds(0, (layers - 1) * strip), :], recv_sem.at[layer_stage])
    strip_rows = rows_of(spot, strip)
    gram[strip_rows, :] = jnp.sum(levels[...], axis=0)

    def share_total(offset, carry):
        index = lax.rem(spot + offset, plane)
        send(gram.at[strip_rows, :], gram.at[strip_rows, :], at_spot(index), share_stage)
        return carry

    lax.fori_loop(1, plane, share_total, 0)
    wait_bytes(part.at[pl.ds(0, (plane - 1) * strip), :], recv_sem.at[share_stage])

    factor_kernel(size, scale, gram, coef_ref, fold, work, inverse)
    mine_fold = jnp.concatenate(
        [fold[slab_of(column, side), :] for column in range(count // count_row)], axis=0
    )

    copies = []
    for turn, (held_ref, owner) in enumerate(((held, me), (twin, partner))):
        if turn:
            own_twin.wait()
            wait_bytes(twin.at[pl.ds(0, (half - 1) * share), :], recv_sem.at[twin_stage])
            wait_bytes(twin.at[pl.ds(0, half * share), :], recv_sem.at[fetch_stage])
        modes[turn] = product(mine_fold, held_ref[...])
        target = out_ref.at[:, columns_of(owner)]
        copy = pltpu.make_async_copy(modes.at[turn, rows_of(place, share), :], target, local_sem.at[2 + turn])
        copy.start()
        copies.append(copy)

        def scatter_modes(offset, carry, turn=turn, target=target):
            index = lax.rem(place + offset, half)
            send(modes.at[turn, rows_of(index, share), :], target, in_half(index), out_stage + turn)
            return carry

        lax.fori_loop(1, half, scatter_modes, 0)

    for copy in copies:
        copy.wait()
    half_bytes = twin.at[pl.ds(0, (half - 1) * share), :]
    for turn in range(2):
        wait_bytes(half_bytes, recv_sem.at[out_stage + turn])
        wait_bytes(half_bytes, send_sem.at[out_stage + turn])
    for chunk in range(chunks):
        wait_bytes(held.at[pl.ds(0, (count - 1) * share), pl.ds(0, piece)], send_sem.at[chunk])
    wait_bytes(half_bytes, send_sem.at[twin_stage])
    wait_bytes(twin.at[pl.ds(0, half * share), :], send_sem.at[fetch_stage])
    wait_bytes(part.at[pl.ds(0, (plane - 1) * strip), :], send_sem.at[scatter_stage])
    wait_bytes(part.at[pl.ds(0, (layers - 1) * strip), :], send_sem.at[layer_stage])
    wait_bytes(part.at[pl.ds(0, (plane - 1) * strip), :], send_sem.at[share_stage])


def eliminate(block):
    size = block.shape[0]
    row_id = lax.broadcasted_iota(jnp.int32, (size, 2 * size), 0)
    col_id = lax.broadcasted_iota(jnp.int32, (size, 2 * size), 1)
    active = jnp.concatenate([block, jnp.zeros_like(block)], axis=1)
    active = jnp.where(col_id == row_id + size, 1.0, active)
    done = []
    for start in range(0, size, GROUP):
        below = row_id[: size - start]
        columns = [
            jnp.broadcast_to(active[:, start + j : start + j + 1], active.shape) for j in range(GROUP)
        ]
        for j in range(GROUP):
            inverse = 1.0 / columns[j][j : j + 1, :]
            ratio = jnp.where(below > j, columns[j] * inverse, 0.0)
            for i in range(j + 1, GROUP):
                columns[i] = columns[i] - ratio * columns[i][j : j + 1, :]
            active = active - ratio * active[j : j + 1, :]
        done.append(active[:GROUP])
        active = active[GROUP:]
    state = jnp.concatenate(done, axis=0)
    pivots = jnp.sum(jnp.where(col_id == row_id, state, 0.0), axis=1, keepdims=True)
    return state[:, size:] * lax.rsqrt(pivots)


def factor_kernel(size, scale, gram_ref, coef_ref, fold_ref, work, inverse):
    total = gram_ref.shape[0]
    blocks = total // size
    work[...] = gram_ref[...]
    inverse[...] = jnp.zeros_like(inverse)
    for k in range(blocks):
        here = slice(k * size, (k + 1) * size)
        low = eliminate(work[here, here])
        before = slice(0, k * size)
        after = slice((k + 1) * size, total)
        if k:
            inverse[here, before] = product(low, inverse[here, before])
        inverse[here, here] = low
        if k < blocks - 1:
            across = product(low, work[here, after])
            down = product(work[after, here], low, NT)
            work[after, after] -= product(down, across)
            inverse[after, slice(0, (k + 1) * size)] -= product(down, inverse[here, slice(0, (k + 1) * size)])
    fold_ref[...] = scale * lax.dot_general(
        coef_ref[...], inverse[...], (((0,), (0,)), ((), ())),
        precision=HIGHEST, preferred_element_type=jnp.float32,
    )


def vmem_spec():
    return pl.BlockSpec(memory_space=pltpu.VMEM)


def any_spec():
    return pl.BlockSpec(memory_space=pl.ANY)


def cost(flops, moved):
    return pl.CostEstimate(flops=flops, bytes_accessed=moved, transcendentals=0)


def factor(gram, coefficients, scale):
    snaps = gram.shape[0]
    return pl.pallas_call(
        functools.partial(factor_kernel, BLOCK, scale),
        out_shape=jax.ShapeDtypeStruct((coefficients.shape[1], snaps), jnp.float32),
        in_specs=[vmem_spec()] * 2,
        out_specs=vmem_spec(),
        scratch_shapes=[pltpu.VMEM((snaps, snaps), jnp.float32)] * 2,
        compiler_params=pltpu.CompilerParams(vmem_limit_bytes=VMEM_BYTES),
        cost_estimate=cost(6 * snaps**3, 12 * snaps**2),
        name="factor",
    )(gram, coefficients)


def direct(snapshots, coefficients, count, count_row):
    share, total_rows = snapshots.shape
    snaps, width = share * count, total_rows // count
    layers = count_row // 2
    plane = count // layers
    strip = snaps // plane
    chunks = 2 if width % 256 == 0 else 1
    square = pltpu.VMEM((snaps, snaps), jnp.float32)
    return pl.pallas_call(
        functools.partial(modes_kernel, count, count_row, chunks, BLOCK, math.sqrt(total_rows)),
        out_shape=jax.ShapeDtypeStruct((share, total_rows), jnp.float32),
        in_specs=[any_spec(), vmem_spec()],
        out_specs=any_spec(),
        scratch_shapes=[
            pltpu.VMEM((snaps, width), jnp.float32),
            pltpu.VMEM((snaps, width), jnp.float32),
            square,
            pltpu.VMEM((plane, strip, snaps), jnp.float32),
            pltpu.VMEM((layers, strip, snaps), jnp.float32),
            square,
            square,
            square,
            square,
            pltpu.VMEM((2, snaps // 2, width), jnp.float32),
            pltpu.SemaphoreType.DMA((4,)),
            pltpu.SemaphoreType.DMA((chunks + 7,)),
            pltpu.SemaphoreType.DMA((chunks + 7,)),
        ],
        compiler_params=pltpu.CompilerParams(
            collective_id=0, has_side_effects=True, vmem_limit_bytes=VMEM_BYTES
        ),
        cost_estimate=cost(4 * snaps * snaps * width, 16 * snaps * width),
        name="modes",
    )(snapshots, coefficients)


def shards(snapshots, coefficients):
    count_row = lax.axis_size("row")
    count = lax.axis_size("read") * count_row
    if snapshots.shape[0] % 8 == 0 and count_row % 4 == 0:
        return direct(snapshots, coefficients, count, count_row)
    held = lax.all_to_all(snapshots, AXES, split_axis=1, concat_axis=0, tiled=True)
    gram = lax.psum(product(held, held, NT), AXES)
    folded = factor(gram, coefficients, math.sqrt(snapshots.shape[1]))
    return lax.all_to_all(product(folded, held), AXES, split_axis=0, concat_axis=1, tiled=True)


def solution(mesh):
    in_specs = (P(AXES, None), P())
    out_specs = P(AXES, None)
    return jax.shard_map(shards, mesh=mesh, in_specs=in_specs, out_specs=out_specs, check_vma=False)
```

```python
import functools
import math

import jax
import jax.numpy as jnp
from jax import lax
from jax.experimental import pallas as pl
from jax.experimental.pallas import tpu as pltpu
from jax.sharding import PartitionSpec as P

AXES = ("read", "row")
HIGHEST = lax.Precision.HIGHEST
NN = (((1,), (0,)), ((), ()))
NT = (((1,), (1,)), ((), ()))
VMEM_BYTES = 60 * 1024 * 1024
GROUP = 16
BLOCK = 64
FETCHED = 640
FETCH = (0, 0)


def product(left, right, dims=NN):
    return lax.dot_general(left, right, dims, precision=HIGHEST, preferred_element_type=jnp.float32)


def coordinates(index, count_row):
    return (lax.div(index, count_row), lax.rem(index, count_row))


def greet(count, count_row, me):
    barrier = pltpu.get_barrier_semaphore()

    def signal(offset, carry):
        other = lax.rem(me + offset, count)
        pl.semaphore_signal(
            barrier, inc=1, device_id=coordinates(other, count_row), device_id_type=pl.DeviceIdType.MESH
        )
        return carry

    lax.fori_loop(1, count, signal, 0)
    return barrier


def wait_bytes(ref, semaphore):
    pltpu.make_async_copy(ref, ref, semaphore).wait()


def modes_kernel(count, count_row, chunks, size, scale, snap_ref, coef_ref, out_ref,
                 held, twin, part, slabs, levels, gram, work, inverse, fold, modes_own, modes_far, modes_twin,
                 local_sem, send_sem, recv_sem):
    share = snap_ref.shape[0]
    snaps, width = held.shape
    fetched = twin.shape[1]
    piece = width // chunks
    half_row = count_row // 2
    half = count // 2
    layers = count_row // 2
    plane = count // layers
    strip = snaps // plane
    read, row = lax.axis_index("read"), lax.axis_index("row")
    me = read * count_row + row
    side = lax.div(row, half_row)
    partner = read * count_row + lax.rem(row + half_row, count_row)
    place = read * half_row + lax.rem(row, half_row)
    layer, core = lax.div(row, 2), lax.rem(row, 2)
    spot = read * 2 + core

    def rows_of(index, length):
        return pl.ds(pl.multiple_of(index * length, length), length)

    def columns_of(index, start=0, size=width):
        return pl.ds(pl.multiple_of(index * width + start, 128), size)

    def in_half(index, which):
        return lax.div(index, half_row) * count_row + which * half_row + lax.rem(index, half_row)

    def mirrored(device):
        other_row = lax.rem(lax.rem(device, count_row) + half_row, count_row)
        return lax.div(device, count_row) * count_row + other_row

    def slab_of(column, which):
        start = (column * count_row + which * half_row) * share
        return pl.ds(pl.multiple_of(start, share), half_row * share)

    def send(source, target, other, stage):
        pltpu.make_async_remote_copy(
            src_ref=source,
            dst_ref=target,
            send_sem=send_sem.at[stage],
            recv_sem=recv_sem.at[stage],
            device_id=coordinates(other, count_row),
            device_id_type=pl.DeviceIdType.MESH,
        ).start()

    mine = rows_of(me, share)
    twin_stage, fetch_stage, scatter_stage, layer_stage, share_stage, out_stage = range(chunks, chunks + 6)
    far_stage, last_stage = out_stage + 1, out_stage + 2

    barrier = greet(count, count_row, me)
    own = pltpu.make_async_copy(snap_ref.at[:, columns_of(me)], held.at[mine, :], local_sem.at[0])
    own.start()
    own_twin = pltpu.make_async_copy(snap_ref.at[:, columns_of(partner, 0, fetched)], twin.at[mine, :], local_sem.at[1])
    own_twin.start()
    pl.semaphore_wait(barrier, count - 1)

    for chunk in range(chunks):
        def scatter(offset, carry, chunk=chunk):
            other = lax.rem(me + offset, count)
            send(
                snap_ref.at[:, pl.ds(pl.multiple_of(other * width + chunk * piece, 128), piece)],
                held.at[mine, pl.ds(chunk * piece, piece)],
                other,
                chunk,
            )
            return carry

        lax.fori_loop(1, count, scatter, 0)

    def scatter_twin(offset, carry):
        other = in_half(lax.rem(place + offset, half), side)
        send(snap_ref.at[:, columns_of(mirrored(other), 0, fetched)], twin.at[mine, :], other, twin_stage)
        return carry

    lax.fori_loop(1, half, scatter_twin, 0)

    own.wait()
    for chunk in range(chunks):
        columns = pl.ds(chunk * piece, piece)
        wait_bytes(held.at[pl.ds(0, (count - 1) * share), columns], recv_sem.at[chunk])
        block = held[:, columns]
        term = product(block, block, NT)
        if chunk:
            part[...] += term
        else:
            part[...] = term

    columns_left = list(range(count // count_row))

    def fetch(number):
        for column in columns_left[:number]:
            slab = slab_of(column, side)
            send(held.at[slab, pl.ds(0, fetched)], twin.at[slab, :], partner, fetch_stage)
        del columns_left[:number]


    slabs[pl.ds(spot, 1)] = part[rows_of(spot, strip), :][None]

    def at_spot(index):
        return lax.div(index, 2) * count_row + layer * 2 + lax.rem(index, 2)

    def scatter_part(offset, carry):
        index = lax.rem(spot + offset, plane)
        send(part.at[rows_of(index, strip), :], slabs.at[spot], at_spot(index), scatter_stage)
        return carry

    lax.fori_loop(1, plane, scatter_part, 0)
    fetch(FETCH[0])
    wait_bytes(part.at[pl.ds(0, (plane - 1) * strip), :], recv_sem.at[scatter_stage])
    levels[pl.ds(layer, 1)] = jnp.sum(slabs[...], axis=0)[None]

    def exchange_layer(offset, carry):
        index = lax.rem(layer + offset, layers)
        send(levels.at[layer], levels.at[layer], read * count_row + index * 2 + core, layer_stage)
        return carry

    lax.fori_loop(1, layers, exchange_layer, 0)
    fetch(FETCH[1])
    wait_bytes(part.at[pl.ds(0, (layers - 1) * strip), :], recv_sem.at[layer_stage])
    strip_rows = rows_of(spot, strip)
    gram[strip_rows, :] = jnp.sum(levels[...], axis=0)

    def share_total(offset, carry):
        index = lax.rem(spot + offset, plane)
        send(gram.at[strip_rows, :], gram.at[strip_rows, :], at_spot(index), share_stage)
        return carry

    lax.fori_loop(1, plane, share_total, 0)
    fetch(len(columns_left))
    wait_bytes(part.at[pl.ds(0, (plane - 1) * strip), :], recv_sem.at[share_stage])

    factor_kernel(size, scale, gram, coef_ref, fold, work, inverse)

    def fold_of(which):
        return jnp.concatenate(
            [fold[slab_of(column, which), :] for column in range(count // count_row)], axis=0
        )

    def scatter_modes(modes, target, which, stage, first):
        def step(offset, carry):
            index = lax.rem(place + offset, half)
            send(modes.at[rows_of(index, share), :], target, in_half(index, which), stage)
            return carry

        lax.fori_loop(first, half, step, 0)

    modes_far[...] = product(fold_of(1 - side), held[:, fetched:])
    scatter_modes(modes_far, out_ref.at[:, columns_of(me, fetched, width - fetched)], 1 - side, far_stage, 0)
    modes_own[...] = product(fold_of(side), held[...])
    target = out_ref.at[:, columns_of(me)]
    keep = pltpu.make_async_copy(modes_own.at[rows_of(place, share), :], target, local_sem.at[2])
    keep.start()
    scatter_modes(modes_own, target, side, out_stage, 1)

    own_twin.wait()
    wait_bytes(twin.at[pl.ds(0, (half - 1) * share), :], recv_sem.at[twin_stage])
    wait_bytes(twin.at[pl.ds(0, half * share), :], recv_sem.at[fetch_stage])
    modes_twin[...] = product(fold_of(side), twin[...])
    target = out_ref.at[:, columns_of(partner, 0, fetched)]
    keep_twin = pltpu.make_async_copy(modes_twin.at[rows_of(place, share), :], target, local_sem.at[3])
    keep_twin.start()
    scatter_modes(modes_twin, target, side, last_stage, 1)

    keep.wait()
    keep_twin.wait()
    for stage, moved in (
        (far_stage, modes_far),
        (out_stage, modes_own.at[pl.ds(0, (half - 1) * share), :]),
        (last_stage, modes_twin.at[pl.ds(0, (half - 1) * share), :]),
    ):
        wait_bytes(moved, recv_sem.at[stage])
        wait_bytes(moved, send_sem.at[stage])
    for chunk in range(chunks):
        wait_bytes(held.at[pl.ds(0, (count - 1) * share), pl.ds(0, piece)], send_sem.at[chunk])
    wait_bytes(twin.at[pl.ds(0, (half - 1) * share), :], send_sem.at[twin_stage])
    wait_bytes(twin.at[pl.ds(0, half * share), :], send_sem.at[fetch_stage])
    wait_bytes(part.at[pl.ds(0, (plane - 1) * strip), :], send_sem.at[scatter_stage])
    wait_bytes(part.at[pl.ds(0, (layers - 1) * strip), :], send_sem.at[layer_stage])
    wait_bytes(part.at[pl.ds(0, (plane - 1) * strip), :], send_sem.at[share_stage])


def eliminate(block):
    size = block.shape[0]
    row_id = lax.broadcasted_iota(jnp.int32, (size, 2 * size), 0)
    col_id = lax.broadcasted_iota(jnp.int32, (size, 2 * size), 1)
    active = jnp.concatenate([block, jnp.zeros_like(block)], axis=1)
    active = jnp.where(col_id == row_id + size, 1.0, active)
    done = []
    for start in range(0, size, GROUP):
        below = row_id[: size - start]
        columns = [
            jnp.broadcast_to(active[:, start + j : start + j + 1], active.shape) for j in range(GROUP)
        ]
        for j in range(GROUP):
            inverse = 1.0 / columns[j][j : j + 1, :]
            ratio = jnp.where(below > j, columns[j] * inverse, 0.0)
            for i in range(j + 1, GROUP):
                columns[i] = columns[i] - ratio * columns[i][j : j + 1, :]
            active = active - ratio * active[j : j + 1, :]
        done.append(active[:GROUP])
        active = active[GROUP:]
    state = jnp.concatenate(done, axis=0)
    pivots = jnp.sum(jnp.where(col_id == row_id, state, 0.0), axis=1, keepdims=True)
    return state[:, size:] * lax.rsqrt(pivots)


def factor_kernel(size, scale, gram_ref, coef_ref, fold_ref, work, inverse):
    total = gram_ref.shape[0]
    blocks = total // size
    work[...] = gram_ref[...]
    inverse[...] = jnp.zeros_like(inverse)
    for k in range(blocks):
        here = slice(k * size, (k + 1) * size)
        low = eliminate(work[here, here])
        before = slice(0, k * size)
        after = slice((k + 1) * size, total)
        if k:
            inverse[here, before] = product(low, inverse[here, before])
        inverse[here, here] = low
        if k < blocks - 1:
            across = product(low, work[here, after])
            down = product(work[after, here], low, NT)
            work[after, after] -= product(down, across)
            inverse[after, slice(0, (k + 1) * size)] -= product(down, inverse[here, slice(0, (k + 1) * size)])
    fold_ref[...] = scale * lax.dot_general(
        coef_ref[...], inverse[...], (((0,), (0,)), ((), ())),
        precision=HIGHEST, preferred_element_type=jnp.float32,
    )


def vmem_spec():
    return pl.BlockSpec(memory_space=pltpu.VMEM)


def any_spec():
    return pl.BlockSpec(memory_space=pl.ANY)


def cost(flops, moved):
    return pl.CostEstimate(flops=flops, bytes_accessed=moved, transcendentals=0)


def factor(gram, coefficients, scale):
    snaps = gram.shape[0]
    return pl.pallas_call(
        functools.partial(factor_kernel, BLOCK, scale),
        out_shape=jax.ShapeDtypeStruct((coefficients.shape[1], snaps), jnp.float32),
        in_specs=[vmem_spec()] * 2,
        out_specs=vmem_spec(),
        scratch_shapes=[pltpu.VMEM((snaps, snaps), jnp.float32)] * 2,
        compiler_params=pltpu.CompilerParams(vmem_limit_bytes=VMEM_BYTES),
        cost_estimate=cost(6 * snaps**3, 12 * snaps**2),
        name="factor",
    )(gram, coefficients)


def direct(snapshots, coefficients, count, count_row):
    share, total_rows = snapshots.shape
    snaps, width = share * count, total_rows // count
    layers = count_row // 2
    plane = count // layers
    strip = snaps // plane
    chunks = 2
    fetched = width * FETCHED // 1280 // 128 * 128
    square = pltpu.VMEM((snaps, snaps), jnp.float32)
    return pl.pallas_call(
        functools.partial(modes_kernel, count, count_row, chunks, BLOCK, math.sqrt(total_rows)),
        out_shape=jax.ShapeDtypeStruct((share, total_rows), jnp.float32),
        in_specs=[any_spec(), vmem_spec()],
        out_specs=any_spec(),
        scratch_shapes=[
            pltpu.VMEM((snaps, width), jnp.float32),
            pltpu.VMEM((snaps, fetched), jnp.float32),
            square,
            pltpu.VMEM((plane, strip, snaps), jnp.float32),
            pltpu.VMEM((layers, strip, snaps), jnp.float32),
            square,
            square,
            square,
            square,
            pltpu.VMEM((snaps // 2, width), jnp.float32),
            pltpu.VMEM((snaps // 2, width - fetched), jnp.float32),
            pltpu.VMEM((snaps // 2, fetched), jnp.float32),
            pltpu.SemaphoreType.DMA((4,)),
            pltpu.SemaphoreType.DMA((chunks + 8,)),
            pltpu.SemaphoreType.DMA((chunks + 8,)),
        ],
        compiler_params=pltpu.CompilerParams(
            collective_id=0, has_side_effects=True, vmem_limit_bytes=VMEM_BYTES
        ),
        cost_estimate=cost(4 * snaps * snaps * width, 16 * snaps * width),
        name="modes",
    )(snapshots, coefficients)


def shards(snapshots, coefficients):
    count_row = lax.axis_size("row")
    count = lax.axis_size("read") * count_row
    if snapshots.shape[0] % 8 == 0 and count_row % 4 == 0 and snapshots.shape[1] % (256 * count) == 0:
        return direct(snapshots, coefficients, count, count_row)
    held = lax.all_to_all(snapshots, AXES, split_axis=1, concat_axis=0, tiled=True)
    gram = lax.psum(product(held, held, NT), AXES)
    folded = factor(gram, coefficients, math.sqrt(snapshots.shape[1]))
    return lax.all_to_all(product(folded, held), AXES, split_axis=0, concat_axis=1, tiled=True)


def solution(mesh):
    in_specs = (P(AXES, None), P())
    out_specs = P(AXES, None)
    return jax.shard_map(shards, mesh=mesh, in_specs=in_specs, out_specs=out_specs, check_vma=False)
```

```python
import functools
import math

import jax
import jax.numpy as jnp
from jax import lax
from jax.experimental import pallas as pl
from jax.experimental.pallas import tpu as pltpu
from jax.sharding import PartitionSpec as P

AXES = ("read", "row")
HIGHEST = lax.Precision.HIGHEST
NN = (((1,), (0,)), ((), ()))
NT = (((1,), (1,)), ((), ()))
VMEM_BYTES = 60 * 1024 * 1024
GROUP = 16
BLOCK = 64
FETCHED = 640
FETCH = (0, 0)


def product(left, right, dims=NN):
    return lax.dot_general(left, right, dims, precision=HIGHEST, preferred_element_type=jnp.float32)


def coordinates(index, count_row):
    return (lax.div(index, count_row), lax.rem(index, count_row))


def greet(count, count_row, me):
    barrier = pltpu.get_barrier_semaphore()

    def signal(offset, carry):
        other = lax.rem(me + offset, count)
        pl.semaphore_signal(
            barrier, inc=1, device_id=coordinates(other, count_row), device_id_type=pl.DeviceIdType.MESH
        )
        return carry

    lax.fori_loop(1, count, signal, 0)
    return barrier


def wait_bytes(ref, semaphore):
    pltpu.make_async_copy(ref, ref, semaphore).wait()


def modes_kernel(count, count_row, chunks, size, scale, snap_ref, coef_ref, out_ref,
                 held, twin, part, slabs, levels, gram, work, inverse, fold, modes_own, modes_far, modes_twin,
                 local_sem, send_sem, recv_sem):
    share = snap_ref.shape[0]
    snaps, width = held.shape
    fetched = twin.shape[1]
    piece = width // chunks
    half_row = count_row // 2
    half = count // 2
    layers = count_row // 2
    plane = count // layers
    strip = snaps // plane
    read, row = lax.axis_index("read"), lax.axis_index("row")
    me = read * count_row + row
    side = lax.div(row, half_row)
    partner = read * count_row + lax.rem(row + half_row, count_row)
    place = read * half_row + lax.rem(row, half_row)
    layer, core = lax.div(row, 2), lax.rem(row, 2)
    spot = read * 2 + core

    def rows_of(index, length):
        return pl.ds(pl.multiple_of(index * length, length), length)

    def columns_of(index, start=0, size=width):
        return pl.ds(pl.multiple_of(index * width + start, 128), size)

    def in_half(index, which):
        return lax.div(index, half_row) * count_row + which * half_row + lax.rem(index, half_row)

    def mirrored(device):
        other_row = lax.rem(lax.rem(device, count_row) + half_row, count_row)
        return lax.div(device, count_row) * count_row + other_row

    def slab_of(column, which):
        start = (column * count_row + which * half_row) * share
        return pl.ds(pl.multiple_of(start, share), half_row * share)

    def send(source, target, other, stage):
        pltpu.make_async_remote_copy(
            src_ref=source,
            dst_ref=target,
            send_sem=send_sem.at[stage],
            recv_sem=recv_sem.at[stage],
            device_id=coordinates(other, count_row),
            device_id_type=pl.DeviceIdType.MESH,
        ).start()

    mine = rows_of(me, share)
    stride = next(step for step in (5, 3, 1) if math.gcd(step, count) == 1)
    twin_stage, fetch_stage, scatter_stage, layer_stage, share_stage, out_stage = range(chunks, chunks + 6)
    far_stage, last_stage = out_stage + 1, out_stage + 2

    barrier = greet(count, count_row, me)
    own = pltpu.make_async_copy(snap_ref.at[:, columns_of(me)], held.at[mine, :], local_sem.at[0])
    own.start()
    own_twin = pltpu.make_async_copy(snap_ref.at[:, columns_of(partner, 0, fetched)], twin.at[mine, :], local_sem.at[1])
    own_twin.start()
    pl.semaphore_wait(barrier, count - 1)

    for chunk in range(chunks):
        def scatter(offset, carry, chunk=chunk):
            other = lax.rem(me + offset * stride, count)
            send(
                snap_ref.at[:, pl.ds(pl.multiple_of(other * width + chunk * piece, 128), piece)],
                held.at[mine, pl.ds(chunk * piece, piece)],
                other,
                chunk,
            )
            return carry

        lax.fori_loop(1, count, scatter, 0)

    def scatter_twin(offset, carry):
        other = in_half(lax.rem(place + offset, half), side)
        send(snap_ref.at[:, columns_of(mirrored(other), 0, fetched)], twin.at[mine, :], other, twin_stage)
        return carry

    lax.fori_loop(1, half, scatter_twin, 0)

    own.wait()
    for chunk in range(chunks):
        columns = pl.ds(chunk * piece, piece)
        wait_bytes(held.at[pl.ds(0, (count - 1) * share), columns], recv_sem.at[chunk])
        block = held[:, columns]
        term = product(block, block, NT)
        if chunk:
            part[...] += term
        else:
            part[...] = term

    columns_left = list(range(count // count_row))

    def fetch(number):
        for column in columns_left[:number]:
            slab = slab_of(column, side)
            send(held.at[slab, pl.ds(0, fetched)], twin.at[slab, :], partner, fetch_stage)
        del columns_left[:number]


    slabs[pl.ds(spot, 1)] = part[rows_of(spot, strip), :][None]

    def at_spot(index):
        return lax.div(index, 2) * count_row + layer * 2 + lax.rem(index, 2)

    def scatter_part(offset, carry):
        index = lax.rem(spot + offset, plane)
        send(part.at[rows_of(index, strip), :], slabs.at[spot], at_spot(index), scatter_stage)
        return carry

    lax.fori_loop(1, plane, scatter_part, 0)
    fetch(FETCH[0])
    wait_bytes(part.at[pl.ds(0, (plane - 1) * strip), :], recv_sem.at[scatter_stage])
    levels[pl.ds(layer, 1)] = jnp.sum(slabs[...], axis=0)[None]

    def exchange_layer(offset, carry):
        index = lax.rem(layer + offset, layers)
        send(levels.at[layer], levels.at[layer], read * count_row + index * 2 + core, layer_stage)
        return carry

    lax.fori_loop(1, layers, exchange_layer, 0)
    fetch(FETCH[1])
    wait_bytes(part.at[pl.ds(0, (layers - 1) * strip), :], recv_sem.at[layer_stage])
    strip_rows = rows_of(spot, strip)
    gram[strip_rows, :] = jnp.sum(levels[...], axis=0)

    def share_total(offset, carry):
        index = lax.rem(spot + offset, plane)
        send(gram.at[strip_rows, :], gram.at[strip_rows, :], at_spot(index), share_stage)
        return carry

    lax.fori_loop(1, plane, share_total, 0)
    fetch(len(columns_left))
    wait_bytes(part.at[pl.ds(0, (plane - 1) * strip), :], recv_sem.at[share_stage])

    factor_kernel(size, scale, gram, coef_ref, fold, work, inverse)

    def fold_of(which):
        return jnp.concatenate(
            [fold[slab_of(column, which), :] for column in range(count // count_row)], axis=0
        )

    def scatter_modes(modes, target, which, stage, first):
        def step(offset, carry):
            index = lax.rem(place + offset, half)
            send(modes.at[rows_of(index, share), :], target, in_half(index, which), stage)
            return carry

        lax.fori_loop(first, half, step, 0)

    modes_far[...] = product(fold_of(1 - side), held[:, fetched:])
    scatter_modes(modes_far, out_ref.at[:, columns_of(me, fetched, width - fetched)], 1 - side, far_stage, 0)
    modes_own[...] = product(fold_of(side), held[...])
    target = out_ref.at[:, columns_of(me)]
    keep = pltpu.make_async_copy(modes_own.at[rows_of(place, share), :], target, local_sem.at[2])
    keep.start()
    scatter_modes(modes_own, target, side, out_stage, 1)

    own_twin.wait()
    wait_bytes(twin.at[pl.ds(0, (half - 1) * share), :], recv_sem.at[twin_stage])
    wait_bytes(twin.at[pl.ds(0, half * share), :], recv_sem.at[fetch_stage])
    modes_twin[...] = product(fold_of(side), twin[...])
    target = out_ref.at[:, columns_of(partner, 0, fetched)]
    keep_twin = pltpu.make_async_copy(modes_twin.at[rows_of(place, share), :], target, local_sem.at[3])
    keep_twin.start()
    scatter_modes(modes_twin, target, side, last_stage, 1)

    keep.wait()
    keep_twin.wait()
    for stage, moved in (
        (far_stage, modes_far),
        (out_stage, modes_own.at[pl.ds(0, (half - 1) * share), :]),
        (last_stage, modes_twin.at[pl.ds(0, (half - 1) * share), :]),
    ):
        wait_bytes(moved, recv_sem.at[stage])
        wait_bytes(moved, send_sem.at[stage])
    for chunk in range(chunks):
        wait_bytes(held.at[pl.ds(0, (count - 1) * share), pl.ds(0, piece)], send_sem.at[chunk])
    wait_bytes(twin.at[pl.ds(0, (half - 1) * share), :], send_sem.at[twin_stage])
    wait_bytes(twin.at[pl.ds(0, half * share), :], send_sem.at[fetch_stage])
    wait_bytes(part.at[pl.ds(0, (plane - 1) * strip), :], send_sem.at[scatter_stage])
    wait_bytes(part.at[pl.ds(0, (layers - 1) * strip), :], send_sem.at[layer_stage])
    wait_bytes(part.at[pl.ds(0, (plane - 1) * strip), :], send_sem.at[share_stage])


def eliminate(block):
    size = block.shape[0]
    row_id = lax.broadcasted_iota(jnp.int32, (size, 2 * size), 0)
    col_id = lax.broadcasted_iota(jnp.int32, (size, 2 * size), 1)
    active = jnp.concatenate([block, jnp.zeros_like(block)], axis=1)
    active = jnp.where(col_id == row_id + size, 1.0, active)
    done = []
    for start in range(0, size, GROUP):
        below = row_id[: size - start]
        columns = [
            jnp.broadcast_to(active[:, start + j : start + j + 1], active.shape) for j in range(GROUP)
        ]
        for j in range(GROUP):
            inverse = 1.0 / columns[j][j : j + 1, :]
            ratio = jnp.where(below > j, columns[j] * inverse, 0.0)
            for i in range(j + 1, GROUP):
                columns[i] = columns[i] - ratio * columns[i][j : j + 1, :]
            active = active - ratio * active[j : j + 1, :]
        done.append(active[:GROUP])
        active = active[GROUP:]
    state = jnp.concatenate(done, axis=0)
    pivots = jnp.sum(jnp.where(col_id == row_id, state, 0.0), axis=1, keepdims=True)
    return state[:, size:] * lax.rsqrt(pivots)


def factor_kernel(size, scale, gram_ref, coef_ref, fold_ref, work, inverse):
    total = gram_ref.shape[0]
    blocks = total // size
    work[...] = gram_ref[...]
    inverse[...] = jnp.zeros_like(inverse)
    for k in range(blocks):
        here = slice(k * size, (k + 1) * size)
        low = eliminate(work[here, here])
        before = slice(0, k * size)
        after = slice((k + 1) * size, total)
        if k:
            inverse[here, before] = product(low, inverse[here, before])
        inverse[here, here] = low
        if k < blocks - 1:
            across = product(low, work[here, after])
            down = product(work[after, here], low, NT)
            work[after, after] -= product(down, across)
            inverse[after, slice(0, (k + 1) * size)] -= product(down, inverse[here, slice(0, (k + 1) * size)])
    fold_ref[...] = scale * lax.dot_general(
        coef_ref[...], inverse[...], (((0,), (0,)), ((), ())),
        precision=HIGHEST, preferred_element_type=jnp.float32,
    )


def vmem_spec():
    return pl.BlockSpec(memory_space=pltpu.VMEM)


def any_spec():
    return pl.BlockSpec(memory_space=pl.ANY)


def cost(flops, moved):
    return pl.CostEstimate(flops=flops, bytes_accessed=moved, transcendentals=0)


def factor(gram, coefficients, scale):
    snaps = gram.shape[0]
    return pl.pallas_call(
        functools.partial(factor_kernel, BLOCK, scale),
        out_shape=jax.ShapeDtypeStruct((coefficients.shape[1], snaps), jnp.float32),
        in_specs=[vmem_spec()] * 2,
        out_specs=vmem_spec(),
        scratch_shapes=[pltpu.VMEM((snaps, snaps), jnp.float32)] * 2,
        compiler_params=pltpu.CompilerParams(vmem_limit_bytes=VMEM_BYTES),
        cost_estimate=cost(6 * snaps**3, 12 * snaps**2),
        name="factor",
    )(gram, coefficients)


def direct(snapshots, coefficients, count, count_row):
    share, total_rows = snapshots.shape
    snaps, width = share * count, total_rows // count
    layers = count_row // 2
    plane = count // layers
    strip = snaps // plane
    chunks = 2
    fetched = width * FETCHED // 1280 // 128 * 128
    square = pltpu.VMEM((snaps, snaps), jnp.float32)
    return pl.pallas_call(
        functools.partial(modes_kernel, count, count_row, chunks, BLOCK, math.sqrt(total_rows)),
        out_shape=jax.ShapeDtypeStruct((share, total_rows), jnp.float32),
        in_specs=[any_spec(), vmem_spec()],
        out_specs=any_spec(),
        scratch_shapes=[
            pltpu.VMEM((snaps, width), jnp.float32),
            pltpu.VMEM((snaps, fetched), jnp.float32),
            square,
            pltpu.VMEM((plane, strip, snaps), jnp.float32),
            pltpu.VMEM((layers, strip, snaps), jnp.float32),
            square,
            square,
            square,
            square,
            pltpu.VMEM((snaps // 2, width), jnp.float32),
            pltpu.VMEM((snaps // 2, width - fetched), jnp.float32),
            pltpu.VMEM((snaps // 2, fetched), jnp.float32),
            pltpu.SemaphoreType.DMA((4,)),
            pltpu.SemaphoreType.DMA((chunks + 8,)),
            pltpu.SemaphoreType.DMA((chunks + 8,)),
        ],
        compiler_params=pltpu.CompilerParams(
            collective_id=0, has_side_effects=True, vmem_limit_bytes=VMEM_BYTES
        ),
        cost_estimate=cost(4 * snaps * snaps * width, 16 * snaps * width),
        name="modes",
    )(snapshots, coefficients)


def shards(snapshots, coefficients):
    count_row = lax.axis_size("row")
    count = lax.axis_size("read") * count_row
    if snapshots.shape[0] % 8 == 0 and count_row % 4 == 0 and snapshots.shape[1] % (256 * count) == 0:
        return direct(snapshots, coefficients, count, count_row)
    held = lax.all_to_all(snapshots, AXES, split_axis=1, concat_axis=0, tiled=True)
    gram = lax.psum(product(held, held, NT), AXES)
    folded = factor(gram, coefficients, math.sqrt(snapshots.shape[1]))
    return lax.all_to_all(product(folded, held), AXES, split_axis=0, concat_axis=1, tiled=True)


def solution(mesh):
    in_specs = (P(AXES, None), P())
    out_specs = P(AXES, None)
    return jax.shard_map(shards, mesh=mesh, in_specs=in_specs, out_specs=out_specs, check_vma=False)
```
